32 devices in a mesh: grp: 2 (over x), img: 16 (over z, y, core).
Axes of the slice: x: 2, y: 2, z: 4, core: 2. Of those that a mesh axis runs over, the one named last changes fastest.
Arguments:
- images: bfloat16 [2048, 3200], P(('grp', 'img')), parts along dimension 0, may hold values from -40 to 40
- projections: bfloat16 [32768, 3200], P(('grp', 'img')), parts along dimension 0, may hold values from -0.21875 to 0.21875
- noise_weight: float32 [6400], P('grp'), parts along dimension 0, may hold values from 0.3 to 3
- owners: int32 [2048, 4], P(('grp', 'img')), parts along dimension 0, may hold values from 0 to 15, all different within a row; in each aligned block of 64 rows (0 to 63, 64 to 127, ...) at most 32 rows name the same one
- counts: int32 [2048], P(('grp', 'img')), parts along dimension 0, may hold values from 2 to 4
Outputs:
- backproj: bfloat16 [32768, 3200], P(('grp', 'img')), parts along dimension 0
- weight_sum: float32 [32768], P(('grp', 'img')), parts along dimension 0
- loglik: float32 [2048], P(('grp', 'img')), parts along dimension 0
The draws below stay inside these ranges and needn't reach their ends.
There are 2 independent parts, one for each index of `grp`. The reference program is written for one: setup_inputs(seed, part) draws one part's arguments, and reference() takes and returns one part's arrays. A program takes and returns all parts, laid end to end along the dimension named above; each array names one. Nothing has to cross between parts.
Inputs may be any that keep to these rules, and one draw needn't show every extreme that they name: `owners`: the 4 blocks named in a row differ; among the rows of one device's 64 images no block is named more than 32 times, and some block is named exactly 32 times. Only the first counts[i] entries of row i of owners are live.
All inputs are finite; a program needn't handle non-finite values.
Results may differ from the reference program's by a relative error of at most 0.001.
The reference program's roundings to bfloat16 on the way (of `weighted` and `posterior`) count: a program that leaves them out, or rounds other values in their place, can miss the bound.
Values may be sent and summed in bfloat16 or wider, within the bound.
A program may use at most 64 MiB of HBM per device.

```python
import math
import jax
import jax.numpy as jnp
import numpy as np
from jax import lax

K = 3200
TILE = 128
TILE_DEV = 8
I_DEV = 64
CAND = 4
CAP = 32
IMAGES = 1024
NDIR = 16384
N_IMG = 16


def draw_images(key, part):
    key = jax.random.fold_in(key, 11)
    first_key = jax.random.fold_in(key, 0)
    values = jnp.clip(jax.random.normal(first_key, (IMAGES, K), jnp.float32), -6.0, 6.0)
    return values.astype(jnp.bfloat16)


def set_ends(drawn, own_key, smallest, high):
    longest = drawn.shape.index(max(drawn.shape))
    spots = []
    for shift in (0, 1):
        where = [jax.random.randint(jax.random.fold_in(own_key, axis), (), 0, length) for axis, length in enumerate(drawn.shape)]
        where[longest] = (where[longest] + shift) % drawn.shape[longest]
        spots.append(tuple(where))
    return drawn.at[spots[0]].set(smallest).at[spots[1]].set(high)


def shard_levels(key, shape, pieces, low, high):
    factor_of, own = 1.0, jax.random.fold_in(key, 6)
    for axis_at, shards_of in pieces:
        draws = jnp.exp(jax.random.uniform(jax.random.fold_in(own, axis_at), (shards_of,), jnp.float32, low / len(pieces), high / len(pieces)))
        factor_of = factor_of * jnp.repeat(draws, shape[axis_at] // shards_of).reshape([-1 if axis == axis_at else 1 for axis in range(len(shape))])
    return factor_of


def deal_out(rng, own, number, rows, count, top, bound, slope):
    sequence = jax.random.permutation(rng, count)
    heavy_load, ordinary = load_shares(count, rows * top, bound, slope, True), load_shares(count, rows * top, bound, slope, False)
    places = jnp.arange(count)

    def named(lengths, rotation):
        used = int((lengths > 0).sum())
        fixed = max(1, used // 4)
        moved = fixed + (places - fixed + rotation * (used - fixed)) % max(1, count - fixed)
        return jnp.zeros((count,), jnp.int32).at[sequence[jnp.where(places < fixed, places, moved)]].set(jnp.asarray(lengths, jnp.int32))

    lengths = jnp.where(number % 4 == 0, named(heavy_load, number // 4), named(ordinary, number - number // 4 - 1))
    mixed = jax.random.permutation(jax.random.fold_in(own, 3), count)
    giver, sink = mixed[0:count // 2 * 2:2], mixed[1:count // 2 * 2:2]
    margin = jnp.minimum(lengths[giver] - 1, bound - lengths[sink]) // 2
    margin = jnp.where((giver == sequence[0]) | (sink == sequence[0]) | (lengths[sink] == 0), 0, jnp.maximum(margin, 0))
    moved = jax.random.randint(jax.random.fold_in(own, 4), (count // 2,), 0, 1 << 20) % (margin + 1)
    lengths = lengths.at[giver].add(-moved).at[sink].add(moved)
    items = jnp.searchsorted(jnp.cumsum(lengths), jnp.arange(rows * top), side="right").astype(jnp.int32)
    listing = items.reshape(top, rows).T
    listing = listing[jax.random.permutation(jax.random.fold_in(own, 1), rows)]
    rotation = jax.random.randint(jax.random.fold_in(own, 2), (rows, 1), 0, top)
    return jnp.take_along_axis(listing, (jnp.arange(top)[None, :] + rotation) % top, axis=1)


def load_shares(number_of, total, limit, skew, full):
    loads = [(1 << 20) // math.isqrt(rank ** skew) + 1 for rank in range(1, number_of + 1)]
    largest = limit if full else min(limit, max(-(-total // number_of), total * loads[0] // sum(loads)))
    least = 1 if total - largest >= number_of - 1 else 0
    given, spare = [largest] + [least] * (number_of - 1), total - largest - least * (number_of - 1)
    while spare > 0:
        movable = [i for i in range(1, number_of) if given[i] < largest] or [i for i in range(1, number_of) if given[i] < limit]
        whole, remaining = sum([loads[i] for i in movable]), spare
        for i in movable:
            more = min(limit - given[i], max(1, remaining * loads[i] // whole), spare)
            given[i] = given[i] + more
            spare = spare - more
    return np.array(given)


def gaussian(rng, shape, width, most, cuts=(), kind=jnp.bfloat16):
    values = jax.random.normal(rng, shape, jnp.float32) * width
    if len(cuts) > 0:
        values = shard_levels(rng, shape, cuts, -0.22, 0.18) * values
    return jnp.clip(values, min=-most, max=most).astype(kind)


def setup_inputs(seed: int = 0, part: int = 0) -> dict:
    key_of = jax.random.split(jax.random.key(seed), 6)
    own_keys = jax.random.split(jax.random.fold_in(key_of[5], part), 6)
    images = draw_images(jax.random.fold_in(jax.random.fold_in(key_of[5], part), 71), part)
    projections = gaussian(own_keys[1], (NDIR, K), (K // 4) ** -0.5, 0.21875, ((0, 16),))
    noise_weight = jnp.clip(jnp.exp(jax.random.uniform(own_keys[2], (K,), jnp.float32, math.log(0.3), math.log(3.0))), 0.3, 3.0)
    owners_keys = jax.random.split(jax.random.fold_in(own_keys[3], 1), IMAGES // I_DEV)
    owners_turns = jax.random.permutation(jax.random.fold_in(own_keys[3], 3), IMAGES // I_DEV)
    owners = jax.vmap(lambda own, number: deal_out(jax.random.fold_in(own_keys[3], 2), own, number, I_DEV, N_IMG, CAND, CAP, 2))(owners_keys, owners_turns).reshape((IMAGES, CAND))
    counts = set_ends(jax.random.randint(own_keys[4], (IMAGES,), 2, CAND + 1), jax.random.fold_in(own_keys[4], 1), 2, CAND).astype(jnp.int32)
    return dict(images=images, projections=projections, noise_weight=noise_weight, owners=owners, counts=counts)


def reference(images, projections, noise_weight, owners, counts):
    devices = N_IMG
    capacity = CAP
    block_dirs = TILE_DEV * TILE
    owner_rows = owners.reshape(devices, I_DEV * CAND)
    one_hot = (owner_rows[:, :, None] == jnp.arange(devices, dtype=jnp.int32)[None, None, :]).astype(jnp.int32)
    earlier = jnp.cumsum(one_hot, axis=1) - one_hot
    within = jnp.sum(earlier * one_hot, axis=2).astype(jnp.int32)
    slot_index = jnp.arange(devices, dtype=jnp.int32)[:, None] * capacity + within
    slot_ids = jnp.arange(IMAGES * CAND, dtype=jnp.int32).reshape(devices, I_DEV * CAND)
    table = jnp.full((devices, devices * capacity), -1, jnp.int32).at[owner_rows, slot_index].set(slot_ids)
    valid = table >= 0
    safe_ids = jnp.maximum(table, 0)
    image_ids = (safe_ids // CAND).astype(jnp.int32)
    proj_wide = projections.astype(jnp.float32)
    weighted = (proj_wide * noise_weight[None, :]).astype(jnp.bfloat16)
    power = jnp.sum(proj_wide * proj_wide * noise_weight[None, :], axis=1)
    weighted_blocks = weighted.reshape(devices, block_dirs, K)
    power_blocks = power.reshape(devices, block_dirs)

    def score_block(inputs):
        block_weighted, block_power, rows_ids = inputs
        gathered = images[rows_ids]
        return jnp.dot(gathered, block_weighted.T, preferred_element_type=jnp.float32) - 0.5 * block_power[None, :]

    score_table = lax.map(score_block, (weighted_blocks, power_blocks, image_ids))
    target = jnp.where(valid, table, IMAGES * CAND).reshape(-1)
    score = jnp.zeros((IMAGES * CAND, block_dirs), jnp.float32).at[target].set(
        score_table.reshape(-1, block_dirs), mode="drop").reshape(IMAGES, CAND, block_dirs)
    live_slot = jnp.arange(CAND, dtype=jnp.int32)[None, :] < counts[:, None]
    peak_score = jnp.max(jnp.where(live_slot[:, :, None], score, -jnp.inf), axis=(1, 2))
    shifted = jnp.where(live_slot[:, :, None], jnp.exp(score - peak_score[:, None, None]), 0.0)
    sum_total = jnp.sum(shifted, axis=(1, 2))
    loglik = peak_score + jnp.log(sum_total)
    posterior = (shifted * (1.0 / sum_total)[:, None, None]).astype(jnp.bfloat16)
    flat_posterior = posterior.reshape(IMAGES * CAND, block_dirs)

    def back_block(inputs):
        rows_ids, post_ids, post_valid = inputs
        weights_here = jnp.where(post_valid[:, None], flat_posterior[post_ids], jnp.zeros((), jnp.bfloat16))
        gathered = images[rows_ids]
        summed = jnp.dot(weights_here.T, gathered, preferred_element_type=jnp.float32)
        return summed.astype(jnp.bfloat16), jnp.sum(weights_here.astype(jnp.float32), axis=0)

    backs, totals = lax.map(back_block, (image_ids, safe_ids, valid))
    return backs.reshape(NDIR, K), totals.reshape(NDIR), loglik
```

```python
import jax
import jax.numpy as jnp
from jax import lax
from jax.experimental import pallas as pl
from jax.experimental.pallas import tpu as pltpu
from jax.sharding import PartitionSpec as P

NZ, NY, NC = 4, 2, 2
PIECES = 2
LOW = -1e30
TILE_ROWS = 512


def gather_and_score(
    images, projections, noise, owners, counts,
    gathered_out, post_out, wsum_out, loglik_out,
    held, weighted, power, scores, post, stats, mask_out, mask_in, masks,
    load_sem, own_sem, send_sem, recv_sem, store_sem, post_sem,
    mask_send, mask_recv, stat_send, stat_recv,
):
    n = NZ * NY * NC
    me = lax.axis_index("img")
    z, y, c = me // (NY * NC), (me // NC) % NY, me % NC
    rows = images.shape[0]
    piece = rows // PIECES
    block_dirs = projections.shape[0]
    tiles = projections.shape[0] // 128
    pair = NC * rows
    chips = NZ * NY

    def place(zs, ys, cs, h):
        start = ((zs * NY + ys) * NC + cs) * rows + h * piece
        return pl.ds(pl.multiple_of(start, piece), piece)

    loads = [
        pltpu.make_async_copy(
            projections.at[pl.ds(t * 128, 128)], weighted.at[pl.ds(t * 128, 128)], load_sem.at[t]
        )
        for t in range(tiles)
    ]
    for load in loads:
        load.start()
    own_rows = pl.ds(pl.multiple_of(me * rows, rows), rows)
    own_load = pltpu.make_async_copy(images, held.at[own_rows], own_sem)
    own_load.start()

    barrier = pltpu.get_barrier_semaphore()
    peers = [lax.rem(me + k, n) for k in range(1, n)]
    for peer in peers:
        pl.semaphore_signal(barrier, inc=1, device_id={"img": peer})
    pl.semaphore_wait(barrier, n - 1)

    def copies(zs, same_line, h, own, toward):
        ys = y if same_line else 1 - y
        at = place(zs, ys, c, h)
        src = images.at[pl.ds(h * piece, piece)] if own else held.at[at]
        chip = zs * NY + ys
        early = jnp.logical_or(zs == 0, zs == NZ - 1) if h == 1 else None

        def copy(way, peer):
            return pltpu.make_async_remote_copy(
                src_ref=src, dst_ref=held.at[at], send_sem=send_sem.at[chip, h, way],
                recv_sem=recv_sem.at[chip * NC + c, h], device_id={"img": peer},
            )

        out = []
        line_ok = None if same_line else early
        if same_line or early is not None:
            for way, step in ((0, 1), (1, -1)):
                if step in toward:
                    ok = z < NZ - 1 if step == 1 else z > 0
                    if line_ok is not None:
                        ok = jnp.logical_and(ok, line_ok)
                    out.append((ok, copy(way, me + step * NY * NC)))
        if same_line:
            if own or early is None:
                ok = None
            else:
                ok = jnp.logical_not(early)
            out.append((ok, copy(2, me + (1 - 2 * y) * NC)))
        out.append((None, copy(3, me + 1 - 2 * c)))
        return out

    def act(items, do):
        for ok, copy in items:
            if ok is None:
                do(copy)
            else:
                @pl.when(ok)
                def _():
                    do(copy)

    def wait_arrival(zs, ys, cs, h):
        at = place(zs, ys, cs, h)
        pltpu.make_async_remote_copy(
            src_ref=held.at[at], dst_ref=held.at[at], send_sem=send_sem.at[0, 0, 0],
            recv_sem=recv_sem.at[(zs * NY + ys) * NC + cs, h], device_id={"img": me},
        ).wait_recv()

    def source(kind):
        side, same_line, d = kind
        zs = z + side * d
        if d == 0:
            return zs, None
        return zs, (zs >= 0) if side < 0 else (zs <= NZ - 1)

    def toward(kind):
        side, same_line, d = kind
        return (1, -1) if d == 0 else (-side,)

    def guarded(ok, body):
        if ok is None:
            body()
        else:
            pl.when(ok)(body)

    def relay(kind, h):
        zs, ok = source(kind)

        def body():
            wait_arrival(zs, y if kind[1] else 1 - y, c, h)
            act(copies(zs, kind[1], h, False, toward(kind)), lambda copy: copy.start())

        guarded(ok, body)

    def settle(kind, h, own):
        zs, ok = source(kind)

        def body():
            act(copies(zs, kind[1], h, own, toward(kind)), lambda copy: copy.wait_send())

        guarded(ok, body)

    OWN = (0, True, 0)
    for h in (1, 0):
        act(copies(z, True, h, True, (1, -1)), lambda copy: copy.start())

    lane = lax.broadcasted_iota(jnp.int32, (rows, 128), 1)
    count = counts[...]
    live = jnp.zeros((rows, 128), jnp.bool_)
    for k in range(owners.shape[1]):
        live = live | ((lane == owners[:, k:k + 1]) & (count > k))
    spot = lax.broadcasted_iota(jnp.int32, (rows, 128), 0) + c * rows
    pick = jnp.where(lane == spot, 1.0, 0.0)
    by_owner = lax.dot_general(
        jnp.where(live, 1.0, 0.0).astype(jnp.bfloat16), pick.astype(jnp.bfloat16),
        (((0,), (0,)), ((), ())), preferred_element_type=jnp.float32,
    )
    for o in range(n):
        mask_out[o] = jnp.broadcast_to(by_owner[o:o + 1, :], (8, 128))
    mask_in[me] = mask_out[me]

    def mask_copy(peer, k):
        return pltpu.make_async_remote_copy(
            src_ref=mask_out.at[peer], dst_ref=mask_in.at[me], send_sem=mask_send.at[k],
            recv_sem=mask_recv.at[me], device_id={"img": peer},
        )

    for k, peer in enumerate(peers):
        mask_copy(peer, k).start()

    width = projections.shape[1]
    for load in loads:
        load.wait()

    def weigh(t, carry):
        r = pl.ds(pl.multiple_of(t * 32, 32), 32)
        total = jnp.zeros((32, 128), jnp.float32)
        for b in range(width // 128):
            cols = pl.ds(b * 128, 128)
            wide = weighted[r, cols].astype(jnp.float32)
            noise_row = noise[:, cols]
            total = total + wide * wide * noise_row
            weighted[r, cols] = (wide * noise_row).astype(jnp.bfloat16)
        power[r, :] = jnp.broadcast_to(
            0.5 * jnp.sum(total, axis=1, keepdims=True), (32, 128)
        )
        return carry

    lax.fori_loop(0, block_dirs // 32, weigh, 0)
    own_load.wait()

    def chunk_rows(ch):
        return pl.ds(pl.multiple_of(ch * pair, pair), pair)

    def store(ch):
        at = chunk_rows(ch)
        return pltpu.make_async_copy(held.at[at], gathered_out.at[at], store_sem.at[ch])

    def score(kind):
        zs, ok = source(kind)
        ys = y if kind[1] else 1 - y

        def body():
            for h in range(PIECES):
                wait_arrival(zs, ys, 1 - c, h)
            ch = zs * NY + ys
            store(ch).start()
            at = chunk_rows(ch)

            def first(t, top):
                r = pl.ds(pl.multiple_of(t * TILE_ROWS, TILE_ROWS), TILE_ROWS)
                s = lax.dot_general(
                    weighted[r, :], held[at, :], (((1,), (1,)), ((), ())),
                    preferred_element_type=jnp.float32,
                ) - power[r, :]
                scores[ch, r, :] = s
                return jnp.maximum(top, jnp.max(s, axis=0, keepdims=True))

            top = lax.fori_loop(
                0, block_dirs // TILE_ROWS, first, jnp.full((1, pair), LOW, jnp.float32)
            )

            def second(t, total):
                r = pl.ds(pl.multiple_of(t * 256, 256), 256)
                e = jnp.exp(scores[ch, r, :] - top)
                scores[ch, r, :] = e
                return total + jnp.sum(e, axis=0, keepdims=True)

            total = lax.fori_loop(
                0, block_dirs // 256, second, jnp.zeros((1, pair), jnp.float32)
            )
            stats[me, 0, pl.ds(ch, 1), :] = top
            stats[me, 1, pl.ds(ch, 1), :] = total

        guarded(ok, body)

    L, R = -1, 1
    ACROSS = (0, False, 0)
    score(OWN)
    relay(ACROSS, 1)
    relay((L, True, 1), 1)
    relay((R, True, 1), 1)
    relay(ACROSS, 0)
    relay((L, True, 1), 0)
    relay((R, True, 1), 0)
    score(ACROSS)
    relay((L, True, 2), 1)
    relay((R, True, 2), 1)
    score((L, True, 1))
    relay((L, True, 2), 0)
    relay((R, True, 2), 0)
    score((R, True, 1))
    for h in (1, 0):
        for side in (L, R):
            relay((side, False, 1), h)
    score((L, True, 2))
    score((R, True, 2))
    for h in (1, 0):
        for side in (L, R):
            relay((side, True, 3), h)
    score((L, False, 1))
    score((R, False, 1))
    for h in (1, 0):
        for side in (L, R):
            relay((side, False, 2), h)
    score((L, True, 3))
    score((R, True, 3))
    score((L, False, 2))
    score((R, False, 2))
    for h in (1, 0):
        for side in (L, R):
            relay((side, False, 3), h)
    score((L, False, 3))
    score((R, False, 3))

    for k, peer in enumerate(peers):
        pltpu.make_async_remote_copy(
            src_ref=mask_in.at[peer], dst_ref=mask_in.at[peer], send_sem=mask_send.at[k],
            recv_sem=mask_recv.at[peer], device_id={"img": me},
        ).wait_recv()
    for ch in range(chips):
        masks[ch:ch + 1, :] = mask_in[ch * NC][0:1, :] + mask_in[ch * NC + 1][0:1, :]
    is_live = masks[...] > 0.5
    top = stats[me, 0]
    stats[me, 0] = jnp.where(is_live, top, LOW)
    stats[me, 1] = jnp.where(is_live, stats[me, 1], 0.0)

    def stat_copy(peer, k):
        return pltpu.make_async_remote_copy(
            src_ref=stats.at[me], dst_ref=stats.at[me], send_sem=stat_send.at[k],
            recv_sem=stat_recv.at[me], device_id={"img": peer},
        )

    for k, peer in enumerate(peers):
        stat_copy(peer, k).start()
    for k, peer in enumerate(peers):
        pltpu.make_async_remote_copy(
            src_ref=stats.at[peer], dst_ref=stats.at[peer], send_sem=stat_send.at[k],
            recv_sem=stat_recv.at[peer], device_id={"img": me},
        ).wait_recv()

    peak = stats[0, 0]
    for o in range(1, n):
        peak = jnp.maximum(peak, stats[o, 0])
    total = jnp.zeros_like(peak)
    for o in range(n):
        total = total + stats[o, 1] * jnp.exp(stats[o, 0] - peak)
    inverse = 1.0 / total
    scale = jnp.where(is_live, jnp.exp(stats[me, 0] - peak) * inverse, 0.0)
    masks[...] = peak + jnp.log(total)
    mine = masks[pl.ds(z * NY + y, 1), :]
    loglik_out[...] = jnp.where(c == 0, mine[:, :rows], mine[:, rows:])

    def post_copy(ch):
        return pltpu.make_async_copy(
            post.at[ch], post_out.at[:, pl.ds(ch * pair, pair)], post_sem.at[ch]
        )

    for ch in range(chips):
        row = scale[ch:ch + 1, :]

        def weights(t, carry):
            r = pl.ds(pl.multiple_of(t * 256, 256), 256)
            p = (scores[ch, r, :] * row).astype(jnp.bfloat16)
            post[ch, r, :] = p
            add = p.astype(jnp.float32)
            power[r, :] = add if ch == 0 else power[r, :] + add
            return carry

        lax.fori_loop(0, block_dirs // 256, weights, 0)
        post_copy(ch).start()
    for t in range(block_dirs // 128):
        turned = jnp.transpose(power[t * 128:(t + 1) * 128, :])
        wsum_out[:, t * 128:(t + 1) * 128] = jnp.sum(turned, axis=0, keepdims=True)

    for h in range(PIECES):
        settle(OWN, h, True)
        settle(ACROSS, h, False)
        for d in range(1, NZ):
            for side in (L, R):
                for line in (True, False):
                    settle((side, line, d), h, False)
    for k, peer in enumerate(peers):
        mask_copy(peer, k).wait_send()
        stat_copy(peer, k).wait_send()
    for ch in range(chips):
        store(ch).wait()
        post_copy(ch).wait()


def line_shards(images, projections, noise_weight, owners, counts):
    rows, width = images.shape
    dirs = projections.shape[0]
    n = NZ * NY * NC
    chips = NZ * NY
    pair = NC * rows
    hbm = pl.BlockSpec(memory_space=pl.ANY)
    vmem = pl.BlockSpec(memory_space=pltpu.VMEM)
    dma = pltpu.SemaphoreType.DMA
    gathered, post, weight_sum, loglik = pl.pallas_call(
        gather_and_score,
        out_shape=(
            jax.ShapeDtypeStruct((n * rows, width), jnp.bfloat16),
            jax.ShapeDtypeStruct((dirs, n * rows), jnp.bfloat16),
            jax.ShapeDtypeStruct((1, dirs), jnp.float32),
            jax.ShapeDtypeStruct((1, rows), jnp.float32),
        ),
        in_specs=[hbm, hbm, vmem, vmem, vmem],
        out_specs=(hbm, hbm, vmem, vmem),
        scratch_shapes=[
            pltpu.VMEM((n * rows, width), jnp.bfloat16),
            pltpu.VMEM((dirs, width), jnp.bfloat16),
            pltpu.VMEM((dirs, 128), jnp.float32),
            pltpu.VMEM((chips, dirs, pair), jnp.float32),
            pltpu.VMEM((chips, dirs, pair), jnp.bfloat16),
            pltpu.VMEM((n, 2, chips, pair), jnp.float32),
            pltpu.VMEM((n, 8, 128), jnp.float32),
            pltpu.VMEM((n, 8, 128), jnp.float32),
            pltpu.VMEM((chips, pair), jnp.float32),
            dma((dirs // 128,)),
            dma(()),
            dma((chips, PIECES, 4)),
            dma((n, PIECES)),
            dma((chips,)),
            dma((chips,)),
            dma((n - 1,)),
            dma((n,)),
            dma((n - 1,)),
            dma((n,)),
        ],
        compiler_params=pltpu.CompilerParams(
            collective_id=0, has_side_effects=True, vmem_limit_bytes=56 * 1024 * 1024
        ),
        cost_estimate=pl.CostEstimate(
            flops=2 * dirs * n * rows * width, bytes_accessed=20_000_000,
            transcendentals=dirs * n * rows,
        ),
        name="gather_and_score",
    )(images, projections, noise_weight.reshape(1, -1), owners, counts.reshape(-1, 1))
    backproj = lax.dot_general(
        post, gathered, (((1,), (0,)), ((), ())), preferred_element_type=jnp.float32
    ).astype(jnp.bfloat16)
    return backproj, weight_sum.reshape(-1), loglik.reshape(-1)


def slot_layout(owners, devices, capacity):
    owner_flat = owners.reshape(-1)
    one_hot = (owner_flat[:, None] == jnp.arange(devices, dtype=jnp.int32)[None, :]).astype(
        jnp.int32
    )
    earlier = jnp.cumsum(one_hot, axis=0) - one_hot
    within = jnp.sum(earlier * one_hot, axis=1)
    return owner_flat * capacity + within


def shards(images, projections, noise_weight, owners, counts):
    devices = lax.axis_size("img")
    local_images, width = images.shape
    candidates = owners.shape[1]
    capacity = 2 * local_images * candidates // devices
    block_dirs = projections.shape[0]
    target = slot_layout(owners, devices, capacity)
    source_rows = jnp.repeat(jnp.arange(local_images, dtype=jnp.int32), candidates)
    outgoing = (
        jnp.zeros((devices * capacity, width), jnp.bfloat16).at[target].set(images[source_rows])
    )
    arrived = lax.all_to_all(
        outgoing.reshape(devices, capacity, width), "img", split_axis=0, concat_axis=0, tiled=True
    ).reshape(devices * capacity, width)
    proj_wide = projections.astype(jnp.float32)
    weighted = (proj_wide * noise_weight[None, :]).astype(jnp.bfloat16)
    power = jnp.sum(proj_wide * proj_wide * noise_weight[None, :], axis=1)
    scores = (
        lax.dot_general(
            arrived, weighted, (((1,), (1,)), ((), ())), preferred_element_type=jnp.float32
        )
        - 0.5 * power[None, :]
    )
    live_slot = jnp.arange(candidates, dtype=jnp.int32)[None, :] < counts[:, None]
    returned = lax.all_to_all(
        scores.reshape(devices, capacity, block_dirs),
        "img",
        split_axis=0,
        concat_axis=0,
        tiled=True,
    ).reshape(devices * capacity, block_dirs)
    mine = returned[target].reshape(local_images, candidates, block_dirs)
    peak_score = jnp.max(jnp.where(live_slot[:, :, None], mine, -jnp.inf), axis=(1, 2))
    shifted = jnp.where(live_slot[:, :, None], jnp.exp(mine - peak_score[:, None, None]), 0.0)
    sum_total = jnp.sum(shifted, axis=(1, 2))
    loglik = peak_score + jnp.log(sum_total)
    posterior = (shifted * (1.0 / sum_total)[:, None, None]).astype(jnp.bfloat16)
    outgoing_post = (
        jnp.zeros((devices * capacity, block_dirs), jnp.bfloat16)
        .at[target]
        .set(posterior.reshape(-1, block_dirs))
    )
    weights_here = lax.all_to_all(
        outgoing_post.reshape(devices, capacity, block_dirs),
        "img",
        split_axis=0,
        concat_axis=0,
        tiled=True,
    ).reshape(devices * capacity, block_dirs)
    backproj = lax.dot_general(
        weights_here, arrived, (((0,), (0,)), ((), ())), preferred_element_type=jnp.float32
    ).astype(jnp.bfloat16)
    weight_sum = jnp.sum(weights_here.astype(jnp.float32), axis=0)
    return (backproj, weight_sum, loglik)


def solution(mesh):
    in_specs = (
        P(("grp", "img"), None),
        P(("grp", "img"), None),
        P("grp"),
        P(("grp", "img"), None),
        P(("grp", "img")),
    )
    out_specs = (P(("grp", "img"), None), P(("grp", "img")), P(("grp", "img")))
    body = line_shards if mesh.shape["img"] == NZ * NY * NC else shards
    return jax.shard_map(body, mesh=mesh, in_specs=in_specs, out_specs=out_specs, check_vma=False)
```

```python
import jax
import jax.numpy as jnp
from jax import lax
from jax.experimental import pallas as pl
from jax.experimental.pallas import tpu as pltpu
from jax.sharding import PartitionSpec as P

NZ, NY, NC = 4, 2, 2
PIECES = 2
LOW = -1e30
TILE_ROWS = 512


def gather_and_score(
    images, projections, noise, owners, counts,
    gathered_out, post_out, loglik_out,
    held, weighted, power, scores, post, local, stats, mask_out, mask_in, masks, lse,
    load_sem, own_sem, send_sem, recv_sem, store_sem, post_sem,
    mask_send, mask_recv, stat_send, stat_recv,
):
    n = NZ * NY * NC
    me = lax.axis_index("img")
    z, y, c = me // (NY * NC), (me // NC) % NY, me % NC
    rows = images.shape[0]
    piece = rows // PIECES
    block_dirs = projections.shape[0]
    tiles = projections.shape[0] // 128
    pair = NC * rows
    chips = NZ * NY

    def place(zs, ys, cs, h):
        start = ((zs * NY + ys) * NC + cs) * rows + h * piece
        return pl.ds(pl.multiple_of(start, piece), piece)

    loads = [
        pltpu.make_async_copy(
            projections.at[pl.ds(t * 128, 128)], weighted.at[pl.ds(t * 128, 128)], load_sem.at[t]
        )
        for t in range(tiles)
    ]
    for load in loads:
        load.start()
    own_rows = pl.ds(pl.multiple_of(me * rows, rows), rows)
    own_load = pltpu.make_async_copy(images, held.at[own_rows], own_sem)
    own_load.start()

    barrier = pltpu.get_barrier_semaphore()
    peers = [lax.rem(me + k, n) for k in range(1, n)]
    for peer in peers:
        pl.semaphore_signal(barrier, inc=1, device_id={"img": peer})
    pl.semaphore_wait(barrier, n - 1)

    def copies(zs, same_line, h, own, toward):
        ys = y if same_line else 1 - y
        at = place(zs, ys, c, h)
        src = images.at[pl.ds(h * piece, piece)] if own else held.at[at]
        chip = zs * NY + ys
        early = jnp.logical_or(zs == 0, zs == NZ - 1) if h == 1 else None

        def copy(way, peer):
            return pltpu.make_async_remote_copy(
                src_ref=src, dst_ref=held.at[at], send_sem=send_sem.at[chip, h, way],
                recv_sem=recv_sem.at[chip * NC + c, h], device_id={"img": peer},
            )

        out = []
        line_ok = None if same_line else early
        if same_line or early is not None:
            for way, step in ((0, 1), (1, -1)):
                if step in toward:
                    ok = z < NZ - 1 if step == 1 else z > 0
                    if line_ok is not None:
                        ok = jnp.logical_and(ok, line_ok)
                    out.append((ok, copy(way, me + step * NY * NC)))
        if same_line:
            if own or early is None:
                ok = None
            else:
                ok = jnp.logical_not(early)
            out.append((ok, copy(2, me + (1 - 2 * y) * NC)))
        out.append((None, copy(3, me + 1 - 2 * c)))
        return out

    def act(items, do):
        for ok, copy in items:
            if ok is None:
                do(copy)
            else:
                @pl.when(ok)
                def _():
                    do(copy)

    def wait_arrival(zs, ys, cs, h):
        at = place(zs, ys, cs, h)
        pltpu.make_async_remote_copy(
            src_ref=held.at[at], dst_ref=held.at[at], send_sem=send_sem.at[0, 0, 0],
            recv_sem=recv_sem.at[(zs * NY + ys) * NC + cs, h], device_id={"img": me},
        ).wait_recv()

    def source(kind):
        side, same_line, d = kind
        zs = z + side * d
        if d == 0:
            return zs, None
        return zs, (zs >= 0) if side < 0 else (zs <= NZ - 1)

    def toward(kind):
        side, same_line, d = kind
        return (1, -1) if d == 0 else (-side,)

    def guarded(ok, body):
        if ok is None:
            body()
        else:
            pl.when(ok)(body)

    def relay(kind, h):
        zs, ok = source(kind)

        def body():
            wait_arrival(zs, y if kind[1] else 1 - y, c, h)
            act(copies(zs, kind[1], h, False, toward(kind)), lambda copy: copy.start())

        guarded(ok, body)

    def settle(kind, h, own):
        zs, ok = source(kind)

        def body():
            act(copies(zs, kind[1], h, own, toward(kind)), lambda copy: copy.wait_send())

        guarded(ok, body)

    local[...] = jnp.zeros_like(local)
    OWN = (0, True, 0)
    for h in (1, 0):
        act(copies(z, True, h, True, (1, -1)), lambda copy: copy.start())

    owner = lax.broadcasted_iota(jnp.int32, (n, rows), 0)
    count = counts[...].reshape(1, rows)
    live = jnp.zeros((n, rows), jnp.float32)
    for k in range(owners.shape[0]):
        live = live + jnp.where((owners[k:k + 1, :] == owner) & (count > k), 1.0, 0.0)
    none = jnp.zeros_like(live)
    by_owner = jnp.concatenate(
        [jnp.where(c == 0, live, none), jnp.where(c == 0, none, live)], axis=1
    )
    for o in range(n):
        mask_out[o] = jnp.broadcast_to(by_owner[o:o + 1, :], (8, 128))
    mask_in[me] = mask_out[me]

    def mask_copy(peer, k):
        return pltpu.make_async_remote_copy(
            src_ref=mask_out.at[peer], dst_ref=mask_in.at[me], send_sem=mask_send.at[k],
            recv_sem=mask_recv.at[me], device_id={"img": peer},
        )

    for k, peer in enumerate(peers):
        mask_copy(peer, k).start()

    width = projections.shape[1]
    for load in loads:
        load.wait()

    def weigh(t, carry):
        r = pl.ds(pl.multiple_of(t * 32, 32), 32)
        total = jnp.zeros((32, 128), jnp.float32)
        for b in range(width // 128):
            cols = pl.ds(b * 128, 128)
            wide = weighted[r, cols].astype(jnp.float32)
            noise_row = noise[cols].reshape(1, 128)
            total = total + wide * wide * noise_row
            weighted[r, cols] = (wide * noise_row).astype(jnp.bfloat16)
        power[r, :] = jnp.broadcast_to(
            0.5 * jnp.sum(total, axis=1, keepdims=True), (32, 128)
        )
        return carry

    lax.fori_loop(0, block_dirs // 32, weigh, 0)
    own_load.wait()

    def chunk_rows(ch):
        return pl.ds(pl.multiple_of(ch * pair, pair), pair)

    def store(ch):
        at = chunk_rows(ch)
        return pltpu.make_async_copy(held.at[at], gathered_out.at[at], store_sem.at[ch])

    def score(kind):
        zs, ok = source(kind)
        ys = y if kind[1] else 1 - y

        def body():
            for h in range(PIECES):
                wait_arrival(zs, ys, 1 - c, h)
            ch = zs * NY + ys
            store(ch).start()
            at = chunk_rows(ch)

            def first(t, top):
                r = pl.ds(pl.multiple_of(t * TILE_ROWS, TILE_ROWS), TILE_ROWS)
                s = lax.dot_general(
                    weighted[r, :], held[at, :], (((1,), (1,)), ((), ())),
                    preferred_element_type=jnp.float32,
                ) - power[r, :]
                scores[ch, r, :] = s
                return jnp.maximum(top, jnp.max(s, axis=0, keepdims=True))

            top = lax.fori_loop(
                0, block_dirs // TILE_ROWS, first, jnp.full((1, pair), LOW, jnp.float32)
            )

            def second(t, total):
                r = pl.ds(pl.multiple_of(t * 256, 256), 256)
                e = jnp.exp(scores[ch, r, :] - top)
                scores[ch, r, :] = e
                return total + jnp.sum(e, axis=0, keepdims=True)

            total = lax.fori_loop(
                0, block_dirs // 256, second, jnp.zeros((1, pair), jnp.float32)
            )
            local[0, pl.ds(ch, 1), :] = top
            local[1, pl.ds(ch, 1), :] = total

        guarded(ok, body)

    def offer(phase):
        if phase == 0:
            for k, peer in enumerate(peers):
                pltpu.make_async_remote_copy(
                    src_ref=mask_in.at[peer], dst_ref=mask_in.at[peer],
                    send_sem=mask_send.at[k], recv_sem=mask_recv.at[peer],
                    device_id={"img": me},
                ).wait_recv()
            for ch in range(chips):
                masks[ch:ch + 1, :] = mask_in[ch * NC][0:1, :] + mask_in[ch * NC + 1][0:1, :]
        is_live = masks[...] > 0.5
        stats[phase, me, 0] = jnp.where(is_live, local[0], LOW)
        stats[phase, me, 1] = jnp.where(is_live, local[1], 0.0)
        for k, peer in enumerate(peers):
            stat_copy(phase, peer, k).start()

    def stat_copy(phase, peer, k):
        return pltpu.make_async_remote_copy(
            src_ref=stats.at[phase, me], dst_ref=stats.at[phase, me],
            send_sem=stat_send.at[phase, k], recv_sem=stat_recv.at[phase, me],
            device_id={"img": peer},
        )

    def post_copy(ch):
        return pltpu.make_async_copy(
            post.at[ch], post_out.at[:, pl.ds(ch * pair, pair)], post_sem.at[ch]
        )

    def conclude(phase, chunks):
        for k, peer in enumerate(peers):
            pltpu.make_async_remote_copy(
                src_ref=stats.at[phase, peer], dst_ref=stats.at[phase, peer],
                send_sem=stat_send.at[phase, k], recv_sem=stat_recv.at[phase, peer],
                device_id={"img": me},
            ).wait_recv()
        peak = stats[phase, 0, 0]
        for o in range(1, n):
            peak = jnp.maximum(peak, stats[phase, o, 0])
        total = jnp.zeros_like(peak)
        for o in range(n):
            total = total + stats[phase, o, 1] * jnp.exp(stats[phase, o, 0] - peak)
        inverse = 1.0 / total
        scale = jnp.where(masks[...] > 0.5, jnp.exp(stats[phase, me, 0] - peak) * inverse, 0.0)
        logs = peak + jnp.log(total)
        for ch in chunks:
            lse[ch:ch + 1, :] = logs[ch:ch + 1, :]
        for ch in chunks:
            row = scale[ch:ch + 1, :]

            def weights(t, carry):
                r = pl.ds(pl.multiple_of(t * 256, 256), 256)
                post[ch, r, :] = (scores[ch, r, :] * row).astype(jnp.bfloat16)
                return carry

            lax.fori_loop(0, block_dirs // 256, weights, 0)
            post_copy(ch).start()

    L, R = -1, 1
    ACROSS = (0, False, 0)
    relay(ACROSS, 1)
    relay((L, True, 1), 1)
    relay((R, True, 1), 1)
    score(OWN)
    relay(ACROSS, 0)
    relay((L, True, 1), 0)
    relay((R, True, 1), 0)
    score(ACROSS)
    relay((L, True, 2), 1)
    relay((R, True, 2), 1)
    score((L, True, 1))
    relay((L, True, 2), 0)
    relay((R, True, 2), 0)
    score((R, True, 1))
    for h in (1, 0):
        for side in (L, R):
            relay((side, False, 1), h)
    score((L, True, 2))
    score((R, True, 2))
    for h in (1, 0):
        for side in (L, R):
            relay((side, True, 3), h)
    score((L, False, 1))
    score((R, False, 1))
    for h in (1, 0):
        for side in (L, R):
            relay((side, False, 2), h)
    score((L, False, 2))
    score((R, False, 2))
    inner = [ch for ch in range(chips) if 0 < ch // NY < NZ - 1]
    outer = [ch for ch in range(chips) if ch not in inner]
    offer(0)
    score((L, True, 3))
    score((R, True, 3))
    for h in range(PIECES):
        settle(OWN, h, True)
        settle(ACROSS, h, False)
        for side in (L, R):
            for line in (True, False):
                settle((side, line, 1), h, False)
    conclude(0, inner)
    for h in (1, 0):
        for side in (L, R):
            relay((side, False, 3), h)
    for h in range(PIECES):
        for side in (L, R):
            settle((side, True, 2), h, False)
            settle((side, False, 2), h, False)
    score((L, False, 3))
    score((R, False, 3))
    offer(1)
    for h in range(PIECES):
        for side in (L, R):
            settle((side, True, 3), h, False)
            settle((side, False, 3), h, False)
    for k, peer in enumerate(peers):
        mask_copy(peer, k).wait_send()
        stat_copy(0, peer, k).wait_send()
    for ch in range(chips):
        store(ch).wait()
    conclude(1, outer)
    mine = lse[pl.ds(z * NY + y, 1), :]
    loglik_out[...] = jnp.where(c == 0, mine[:, :rows], mine[:, rows:]).reshape(rows)
    for k, peer in enumerate(peers):
        stat_copy(1, peer, k).wait_send()
    for ch in range(chips):
        post_copy(ch).wait()


BACK_COLS = 512


def back(post, gathered, loglik, out, wsum_out, loglik_out, weights, held, total, sems, out_sems):
    dirs, depth = weights.shape
    width = held.shape[1]
    spans = [(b, min(BACK_COLS, width - b)) for b in range(0, width, BACK_COLS)]
    first = pltpu.make_async_copy(post, weights, sems.at[len(spans)])
    first.start()
    loads, saves = [], []
    for j, (b, size) in enumerate(spans):
        cols = pl.ds(b, size)
        loads.append(pltpu.make_async_copy(gathered.at[:, cols], held.at[:, cols], sems.at[j]))
        saves.append(pltpu.make_async_copy(total.at[:, cols], out.at[:, cols], out_sems.at[j]))
    for load in loads:
        load.start()
    loglik_out[...] = loglik[...]
    first.wait()
    for j, (b, size) in enumerate(spans):
        loads[j].wait()

        def tile(t, carry):
            r = pl.ds(pl.multiple_of(t * 256, 256), 256)
            total[r, b:b + size] = jnp.dot(
                weights[r, :], held[:, b:b + size], preferred_element_type=jnp.float32
            ).astype(jnp.bfloat16)
            return carry

        lax.fori_loop(0, dirs // 256, tile, 0)
        saves[j].start()
        if j == 0:
            for t in range(dirs // 128):
                part = jnp.zeros((128, 128), jnp.float32)
                for k in range(depth // 128):
                    part = part + weights[t * 128:(t + 1) * 128, k * 128:(k + 1) * 128].astype(
                        jnp.float32
                    )
                wsum_out[t * 128:(t + 1) * 128] = jnp.sum(jnp.transpose(part), axis=0)
    for save in saves:
        save.wait()


def line_shards(images, projections, noise_weight, owners, counts):
    rows, width = images.shape
    dirs = projections.shape[0]
    n = NZ * NY * NC
    chips = NZ * NY
    pair = NC * rows
    hbm = pl.BlockSpec(memory_space=pl.ANY)
    vmem = pl.BlockSpec(memory_space=pltpu.VMEM)
    dma = pltpu.SemaphoreType.DMA
    gathered, post, loglik = pl.pallas_call(
        gather_and_score,
        out_shape=(
            jax.ShapeDtypeStruct((n * rows, width), jnp.bfloat16),
            jax.ShapeDtypeStruct((dirs, n * rows), jnp.bfloat16),
            jax.ShapeDtypeStruct((rows,), jnp.float32),
        ),
        in_specs=[hbm, hbm, vmem, vmem, vmem],
        out_specs=(hbm, hbm, vmem),
        scratch_shapes=[
            pltpu.VMEM((n * rows, width), jnp.bfloat16),
            pltpu.VMEM((dirs, width), jnp.bfloat16),
            pltpu.VMEM((dirs, 128), jnp.float32),
            pltpu.VMEM((chips, dirs, pair), jnp.float32),
            pltpu.VMEM((chips, dirs, pair), jnp.bfloat16),
            pltpu.VMEM((2, chips, pair), jnp.float32),
            pltpu.VMEM((2, n, 2, chips, pair), jnp.float32),
            pltpu.VMEM((n, 8, 128), jnp.float32),
            pltpu.VMEM((n, 8, 128), jnp.float32),
            pltpu.VMEM((chips, pair), jnp.float32),
            pltpu.VMEM((chips, pair), jnp.float32),
            dma((dirs // 128,)),
            dma(()),
            dma((chips, PIECES, 4)),
            dma((n, PIECES)),
            dma((chips,)),
            dma((chips,)),
            dma((n - 1,)),
            dma((n,)),
            dma((2, n - 1)),
            dma((2, n)),
        ],
        compiler_params=pltpu.CompilerParams(
            collective_id=0, has_side_effects=True, vmem_limit_bytes=56 * 1024 * 1024
        ),
        cost_estimate=pl.CostEstimate(
            flops=2 * dirs * n * rows * width, bytes_accessed=20_000_000,
            transcendentals=dirs * n * rows,
        ),
        name="gather_and_score",
    )(images, projections, noise_weight, owners.T, counts)
    spans = -(-width // BACK_COLS)
    return pl.pallas_call(
        back,
        out_shape=(
            jax.ShapeDtypeStruct((dirs, width), jnp.bfloat16),
            jax.ShapeDtypeStruct((dirs,), jnp.float32),
            jax.ShapeDtypeStruct((rows,), jnp.float32),
        ),
        in_specs=[hbm, hbm, vmem],
        out_specs=(hbm, vmem, vmem),
        scratch_shapes=[
            pltpu.VMEM((dirs, n * rows), jnp.bfloat16),
            pltpu.VMEM((n * rows, width), jnp.bfloat16),
            pltpu.VMEM((dirs, width), jnp.bfloat16),
            dma((spans + 1,)),
            dma((spans,)),
        ],
        compiler_params=pltpu.CompilerParams(vmem_limit_bytes=56 * 1024 * 1024),
        cost_estimate=pl.CostEstimate(
            flops=2 * dirs * n * rows * width, bytes_accessed=16_000_000, transcendentals=0
        ),
        name="back",
    )(post, gathered, loglik)


def slot_layout(owners, devices, capacity):
    owner_flat = owners.reshape(-1)
    one_hot = (owner_flat[:, None] == jnp.arange(devices, dtype=jnp.int32)[None, :]).astype(
        jnp.int32
    )
    earlier = jnp.cumsum(one_hot, axis=0) - one_hot
    within = jnp.sum(earlier * one_hot, axis=1)
    return owner_flat * capacity + within


def shards(images, projections, noise_weight, owners, counts):
    devices = lax.axis_size("img")
    local_images, width = images.shape
    candidates = owners.shape[1]
    capacity = 2 * local_images * candidates // devices
    block_dirs = projections.shape[0]
    target = slot_layout(owners, devices, capacity)
    source_rows = jnp.repeat(jnp.arange(local_images, dtype=jnp.int32), candidates)
    outgoing = (
        jnp.zeros((devices * capacity, width), jnp.bfloat16).at[target].set(images[source_rows])
    )
    arrived = lax.all_to_all(
        outgoing.reshape(devices, capacity, width), "img", split_axis=0, concat_axis=0, tiled=True
    ).reshape(devices * capacity, width)
    proj_wide = projections.astype(jnp.float32)
    weighted = (proj_wide * noise_weight[None, :]).astype(jnp.bfloat16)
    power = jnp.sum(proj_wide * proj_wide * noise_weight[None, :], axis=1)
    scores = (
        lax.dot_general(
            arrived, weighted, (((1,), (1,)), ((), ())), preferred_element_type=jnp.float32
        )
        - 0.5 * power[None, :]
    )
    live_slot = jnp.arange(candidates, dtype=jnp.int32)[None, :] < counts[:, None]
    returned = lax.all_to_all(
        scores.reshape(devices, capacity, block_dirs),
        "img",
        split_axis=0,
        concat_axis=0,
        tiled=True,
    ).reshape(devices * capacity, block_dirs)
    mine = returned[target].reshape(local_images, candidates, block_dirs)
    peak_score = jnp.max(jnp.where(live_slot[:, :, None], mine, -jnp.inf), axis=(1, 2))
    shifted = jnp.where(live_slot[:, :, None], jnp.exp(mine - peak_score[:, None, None]), 0.0)
    sum_total = jnp.sum(shifted, axis=(1, 2))
    loglik = peak_score + jnp.log(sum_total)
    posterior = (shifted * (1.0 / sum_total)[:, None, None]).astype(jnp.bfloat16)
    outgoing_post = (
        jnp.zeros((devices * capacity, block_dirs), jnp.bfloat16)
        .at[target]
        .set(posterior.reshape(-1, block_dirs))
    )
    weights_here = lax.all_to_all(
        outgoing_post.reshape(devices, capacity, block_dirs),
        "img",
        split_axis=0,
        concat_axis=0,
        tiled=True,
    ).reshape(devices * capacity, block_dirs)
    backproj = lax.dot_general(
        weights_here, arrived, (((0,), (0,)), ((), ())), preferred_element_type=jnp.float32
    ).astype(jnp.bfloat16)
    weight_sum = jnp.sum(weights_here.astype(jnp.float32), axis=0)
    return (backproj, weight_sum, loglik)


def solution(mesh):
    in_specs = (
        P(("grp", "img"), None),
        P(("grp", "img"), None),
        P("grp"),
        P(("grp", "img"), None),
        P(("grp", "img")),
    )
    out_specs = (P(("grp", "img"), None), P(("grp", "img")), P(("grp", "img")))
    body = line_shards if mesh.shape["img"] == NZ * NY * NC else shards
    return jax.shard_map(body, mesh=mesh, in_specs=in_specs, out_specs=out_specs, check_vma=False)
```

```python
import jax
import jax.numpy as jnp
from jax import lax
from jax.experimental import pallas as pl
from jax.experimental.pallas import tpu as pltpu
from jax.sharding import PartitionSpec as P

NZ, NY, NC = 4, 2, 2
PIECES = 2
LOW = -1e30
TILE_ROWS = 1024


def gather_and_score(
    images, projections, noise, owners, counts,
    gathered_out, post_out, loglik_out,
    held, weighted, power, scores, post, local, stats, mask_out, mask_in, masks, lse,
    load_sem, own_sem, send_sem, recv_sem, store_sem, post_sem,
    mask_send, mask_recv, stat_send, stat_recv,
):
    n = NZ * NY * NC
    me = lax.axis_index("img")
    z, y, c = me // (NY * NC), (me // NC) % NY, me % NC
    rows = images.shape[0]
    piece = rows // PIECES
    block_dirs = projections.shape[0]
    tiles = projections.shape[0] // 128
    pair = NC * rows
    chips = NZ * NY

    def place(zs, ys, cs, h):
        start = ((zs * NY + ys) * NC + cs) * rows + h * piece
        return pl.ds(pl.multiple_of(start, piece), piece)

    loads = [
        pltpu.make_async_copy(
            projections.at[pl.ds(t * 128, 128)], weighted.at[pl.ds(t * 128, 128)], load_sem.at[t]
        )
        for t in range(tiles)
    ]
    for load in loads:
        load.start()
    own_rows = pl.ds(pl.multiple_of(me * rows, rows), rows)
    own_load = pltpu.make_async_copy(images, held.at[own_rows], own_sem)
    own_load.start()

    barrier = pltpu.get_barrier_semaphore()
    peers = [lax.rem(me + k, n) for k in range(1, n)]
    for peer in peers:
        pl.semaphore_signal(barrier, inc=1, device_id={"img": peer})
    pl.semaphore_wait(barrier, n - 1)

    def copies(zs, same_line, h, own, toward):
        ys = y if same_line else 1 - y
        at = place(zs, ys, c, h)
        src = images.at[pl.ds(h * piece, piece)] if own else held.at[at]
        chip = zs * NY + ys
        early = jnp.logical_or(zs == 0, zs == NZ - 1) if h == 1 else None

        def copy(way, peer):
            return pltpu.make_async_remote_copy(
                src_ref=src, dst_ref=held.at[at], send_sem=send_sem.at[chip, h, way],
                recv_sem=recv_sem.at[chip * NC + c, h], device_id={"img": peer},
            )

        out = []
        line_ok = None if same_line else early
        if same_line or early is not None:
            for way, step in ((0, 1), (1, -1)):
                if step in toward:
                    ok = z < NZ - 1 if step == 1 else z > 0
                    if line_ok is not None:
                        ok = jnp.logical_and(ok, line_ok)
                    out.append((ok, copy(way, me + step * NY * NC)))
        if same_line:
            if own or early is None:
                ok = None
            else:
                ok = jnp.logical_not(early)
            out.append((ok, copy(2, me + (1 - 2 * y) * NC)))
        out.append((None, copy(3, me + 1 - 2 * c)))
        return out

    def act(items, do):
        for ok, copy in items:
            if ok is None:
                do(copy)
            else:
                @pl.when(ok)
                def _():
                    do(copy)

    def wait_arrival(zs, ys, cs, h):
        at = place(zs, ys, cs, h)
        pltpu.make_async_remote_copy(
            src_ref=held.at[at], dst_ref=held.at[at], send_sem=send_sem.at[0, 0, 0],
            recv_sem=recv_sem.at[(zs * NY + ys) * NC + cs, h], device_id={"img": me},
        ).wait_recv()

    def source(kind):
        side, same_line, d = kind
        zs = z + side * d
        if d == 0:
            return zs, None
        return zs, (zs >= 0) if side < 0 else (zs <= NZ - 1)

    def toward(kind):
        side, same_line, d = kind
        return (1, -1) if d == 0 else (-side,)

    def guarded(ok, body):
        if ok is None:
            body()
        else:
            pl.when(ok)(body)

    def relay(kind, h):
        zs, ok = source(kind)

        def body():
            wait_arrival(zs, y if kind[1] else 1 - y, c, h)
            act(copies(zs, kind[1], h, False, toward(kind)), lambda copy: copy.start())

        guarded(ok, body)

    def settle(kind, h, own):
        zs, ok = source(kind)

        def body():
            act(copies(zs, kind[1], h, own, toward(kind)), lambda copy: copy.wait_send())

        guarded(ok, body)

    local[...] = jnp.zeros_like(local)
    OWN = (0, True, 0)
    for h in (1, 0):
        act(copies(z, True, h, True, (1, -1)), lambda copy: copy.start())

    owner = lax.broadcasted_iota(jnp.int32, (n, rows), 0)
    count = counts[...].reshape(1, rows)
    live = jnp.zeros((n, rows), jnp.float32)
    for k in range(owners.shape[0]):
        live = live + jnp.where((owners[k:k + 1, :] == owner) & (count > k), 1.0, 0.0)
    none = jnp.zeros_like(live)
    by_owner = jnp.concatenate(
        [jnp.where(c == 0, live, none), jnp.where(c == 0, none, live)], axis=1
    )
    for o in range(n):
        mask_out[o] = jnp.broadcast_to(by_owner[o:o + 1, :], (8, 128))
    mask_in[me] = mask_out[me]

    def mask_copy(peer, k):
        return pltpu.make_async_remote_copy(
            src_ref=mask_out.at[peer], dst_ref=mask_in.at[me], send_sem=mask_send.at[k],
            recv_sem=mask_recv.at[me], device_id={"img": peer},
        )

    for k, peer in enumerate(peers):
        mask_copy(peer, k).start()

    width = projections.shape[1]
    for load in loads:
        load.wait()

    def weigh(t, carry):
        r = pl.ds(pl.multiple_of(t * 32, 32), 32)
        total = jnp.zeros((32, 128), jnp.float32)
        for b in range(width // 128):
            cols = pl.ds(b * 128, 128)
            wide = weighted[r, cols].astype(jnp.float32)
            noise_row = noise[cols].reshape(1, 128)
            total = total + wide * wide * noise_row
            weighted[r, cols] = (wide * noise_row).astype(jnp.bfloat16)
        power[r, :] = jnp.broadcast_to(
            0.5 * jnp.sum(total, axis=1, keepdims=True), (32, 128)
        )
        return carry

    lax.fori_loop(0, block_dirs // 32, weigh, 0)
    own_load.wait()

    def chunk_rows(ch):
        return pl.ds(pl.multiple_of(ch * pair, pair), pair)

    def store(ch):
        at = chunk_rows(ch)
        return pltpu.make_async_copy(held.at[at], gathered_out.at[at], store_sem.at[ch])

    def score(kind):
        zs, ok = source(kind)
        ys = y if kind[1] else 1 - y

        def body():
            for h in range(PIECES):
                wait_arrival(zs, ys, 1 - c, h)
            ch = zs * NY + ys
            store(ch).start()
            at = chunk_rows(ch)

            def first(t, top):
                r = pl.ds(pl.multiple_of(t * TILE_ROWS, TILE_ROWS), TILE_ROWS)
                s = lax.dot_general(
                    weighted[r, :], held[at, :], (((1,), (1,)), ((), ())),
                    preferred_element_type=jnp.float32,
                ) - power[r, :]
                scores[ch, r, :] = s
                return jnp.maximum(top, jnp.max(s, axis=0, keepdims=True))

            top = lax.fori_loop(
                0, block_dirs // TILE_ROWS, first, jnp.full((1, pair), LOW, jnp.float32)
            )

            def second(t, total):
                r = pl.ds(pl.multiple_of(t * 256, 256), 256)
                e = jnp.exp(scores[ch, r, :] - top)
                scores[ch, r, :] = e
                return total + jnp.sum(e, axis=0, keepdims=True)

            total = lax.fori_loop(
                0, block_dirs // 256, second, jnp.zeros((1, pair), jnp.float32)
            )
            local[0, pl.ds(ch, 1), :] = top
            local[1, pl.ds(ch, 1), :] = total

        guarded(ok, body)

    def offer():
        for k, peer in enumerate(peers):
            pltpu.make_async_remote_copy(
                src_ref=mask_in.at[peer], dst_ref=mask_in.at[peer],
                send_sem=mask_send.at[k], recv_sem=mask_recv.at[peer],
                device_id={"img": me},
            ).wait_recv()
        for ch in range(chips):
            masks[ch:ch + 1, :] = mask_in[ch * NC][0:1, :] + mask_in[ch * NC + 1][0:1, :]
        is_live = masks[...] > 0.5
        stats[me, 0] = jnp.where(is_live, local[0], LOW)
        stats[me, 1] = jnp.where(is_live, local[1], 0.0)
        for k, peer in enumerate(peers):
            stat_copy(peer, k).start()

    def stat_copy(peer, k):
        return pltpu.make_async_remote_copy(
            src_ref=stats.at[me], dst_ref=stats.at[me],
            send_sem=stat_send.at[k], recv_sem=stat_recv.at[me],
            device_id={"img": peer},
        )

    def post_copy(ch):
        return pltpu.make_async_copy(
            post.at[ch], post_out.at[:, pl.ds(ch * pair, pair)], post_sem.at[ch]
        )

    def conclude(chunks):
        for k, peer in enumerate(peers):
            pltpu.make_async_remote_copy(
                src_ref=stats.at[peer], dst_ref=stats.at[peer],
                send_sem=stat_send.at[k], recv_sem=stat_recv.at[peer],
                device_id={"img": me},
            ).wait_recv()
        peak = stats[0, 0]
        for o in range(1, n):
            peak = jnp.maximum(peak, stats[o, 0])
        total = jnp.zeros_like(peak)
        for o in range(n):
            total = total + stats[o, 1] * jnp.exp(stats[o, 0] - peak)
        inverse = 1.0 / total
        scale = jnp.where(masks[...] > 0.5, jnp.exp(stats[me, 0] - peak) * inverse, 0.0)
        logs = peak + jnp.log(total)
        for ch in chunks:
            lse[ch:ch + 1, :] = logs[ch:ch + 1, :]
        for ch in chunks:
            row = scale[ch:ch + 1, :]

            def weights(t, carry):
                r = pl.ds(pl.multiple_of(t * 256, 256), 256)
                post[ch, r, :] = (scores[ch, r, :] * row).astype(jnp.bfloat16)
                return carry

            lax.fori_loop(0, block_dirs // 256, weights, 0)
            post_copy(ch).start()

    L, R = -1, 1
    ACROSS = (0, False, 0)
    relay(ACROSS, 1)
    relay((L, True, 1), 1)
    relay((R, True, 1), 1)
    score(OWN)
    relay(ACROSS, 0)
    relay((L, True, 1), 0)
    relay((R, True, 1), 0)
    score(ACROSS)
    relay((L, True, 2), 1)
    relay((R, True, 2), 1)
    score((L, True, 1))
    relay((L, True, 2), 0)
    relay((R, True, 2), 0)
    score((R, True, 1))
    for h in (1, 0):
        for side in (L, R):
            relay((side, False, 1), h)
    score((L, True, 2))
    score((R, True, 2))
    for h in (1, 0):
        for side in (L, R):
            relay((side, True, 3), h)
    score((L, False, 1))
    score((R, False, 1))
    for h in (1, 0):
        for side in (L, R):
            relay((side, False, 2), h)
    score((L, False, 2))
    score((R, False, 2))
    score((L, True, 3))
    score((R, True, 3))
    for h in (1, 0):
        for side in (L, R):
            relay((side, False, 3), h)
    for h in range(PIECES):
        settle(OWN, h, True)
        settle(ACROSS, h, False)
        for d in (1, 2):
            for side in (L, R):
                for line in (True, False):
                    settle((side, line, d), h, False)
    score((L, False, 3))
    score((R, False, 3))
    offer()
    for h in range(PIECES):
        for side in (L, R):
            settle((side, True, 3), h, False)
            settle((side, False, 3), h, False)
    for k, peer in enumerate(peers):
        mask_copy(peer, k).wait_send()
    for ch in range(chips):
        store(ch).wait()
    conclude(range(chips))
    mine = lse[pl.ds(z * NY + y, 1), :]
    loglik_out[...] = jnp.where(c == 0, mine[:, :rows], mine[:, rows:]).reshape(rows)
    for k, peer in enumerate(peers):
        stat_copy(peer, k).wait_send()
    for ch in range(chips):
        post_copy(ch).wait()


BACK_ROWS, BACK_COLS = 512, 512


def back(post, gathered, loglik, out, wsum_out, loglik_out, weights, held, total, sems, out_sems):
    dirs, depth = weights.shape
    width = held.shape[1]
    spans = [(b, min(BACK_COLS, width - b)) for b in range(0, width, BACK_COLS)]
    first = pltpu.make_async_copy(post, weights, sems.at[len(spans)])
    first.start()
    loads, saves = [], []
    for j, (b, size) in enumerate(spans):
        cols = pl.ds(b, size)
        loads.append(pltpu.make_async_copy(gathered.at[:, cols], held.at[:, cols], sems.at[j]))
        saves.append(pltpu.make_async_copy(total.at[:, cols], out.at[:, cols], out_sems.at[j]))
    for load in loads:
        load.start()
    loglik_out[...] = loglik[...]
    first.wait()
    for j, (b, size) in enumerate(spans):
        loads[j].wait()

        for t in range(0, dirs, BACK_ROWS):
            total[t:t + BACK_ROWS, b:b + size] = jnp.dot(
                weights[t:t + BACK_ROWS, :], held[:, b:b + size],
                preferred_element_type=jnp.float32,
            ).astype(jnp.bfloat16)
        saves[j].start()
    for t in range(dirs // 128):
        part = jnp.zeros((128, 128), jnp.float32)
        for k in range(depth // 128):
            part = part + weights[t * 128:(t + 1) * 128, k * 128:(k + 1) * 128].astype(jnp.float32)
        wsum_out[t * 128:(t + 1) * 128] = jnp.sum(jnp.transpose(part), axis=0)
    for save in saves:
        save.wait()


def line_shards(images, projections, noise_weight, owners, counts):
    rows, width = images.shape
    dirs = projections.shape[0]
    n = NZ * NY * NC
    chips = NZ * NY
    pair = NC * rows
    hbm = pl.BlockSpec(memory_space=pl.ANY)
    vmem = pl.BlockSpec(memory_space=pltpu.VMEM)
    dma = pltpu.SemaphoreType.DMA
    gathered, post, loglik = pl.pallas_call(
        gather_and_score,
        out_shape=(
            jax.ShapeDtypeStruct((n * rows, width), jnp.bfloat16),
            jax.ShapeDtypeStruct((dirs, n * rows), jnp.bfloat16),
            jax.ShapeDtypeStruct((rows,), jnp.float32),
        ),
        in_specs=[hbm, hbm, vmem, vmem, vmem],
        out_specs=(hbm, hbm, vmem),
        scratch_shapes=[
            pltpu.VMEM((n * rows, width), jnp.bfloat16),
            pltpu.VMEM((dirs, width), jnp.bfloat16),
            pltpu.VMEM((dirs, 128), jnp.float32),
            pltpu.VMEM((chips, dirs, pair), jnp.float32),
            pltpu.VMEM((chips, dirs, pair), jnp.bfloat16),
            pltpu.VMEM((2, chips, pair), jnp.float32),
            pltpu.VMEM((n, 2, chips, pair), jnp.float32),
            pltpu.VMEM((n, 8, 128), jnp.float32),
            pltpu.VMEM((n, 8, 128), jnp.float32),
            pltpu.VMEM((chips, pair), jnp.float32),
            pltpu.VMEM((chips, pair), jnp.float32),
            dma((dirs // 128,)),
            dma(()),
            dma((chips, PIECES, 4)),
            dma((n, PIECES)),
            dma((chips,)),
            dma((chips,)),
            dma((n - 1,)),
            dma((n,)),
            dma((n - 1,)),
            dma((n,)),
        ],
        compiler_params=pltpu.CompilerParams(
            collective_id=0, has_side_effects=True, vmem_limit_bytes=56 * 1024 * 1024
        ),
        cost_estimate=pl.CostEstimate(
            flops=2 * dirs * n * rows * width, bytes_accessed=20_000_000,
            transcendentals=dirs * n * rows,
        ),
        name="gather_and_score",
    )(images, projections, noise_weight, owners.T, counts)
    spans = -(-width // BACK_COLS)
    return pl.pallas_call(
        back,
        out_shape=(
            jax.ShapeDtypeStruct((dirs, width), jnp.bfloat16),
            jax.ShapeDtypeStruct((dirs,), jnp.float32),
            jax.ShapeDtypeStruct((rows,), jnp.float32),
        ),
        in_specs=[hbm, hbm, vmem],
        out_specs=(hbm, vmem, vmem),
        scratch_shapes=[
            pltpu.VMEM((dirs, n * rows), jnp.bfloat16),
            pltpu.VMEM((n * rows, width), jnp.bfloat16),
            pltpu.VMEM((dirs, width), jnp.bfloat16),
            dma((spans + 1,)),
            dma((spans,)),
        ],
        compiler_params=pltpu.CompilerParams(vmem_limit_bytes=56 * 1024 * 1024),
        cost_estimate=pl.CostEstimate(
            flops=2 * dirs * n * rows * width, bytes_accessed=16_000_000, transcendentals=0
        ),
        name="back",
    )(post, gathered, loglik)


def slot_layout(owners, devices, capacity):
    owner_flat = owners.reshape(-1)
    one_hot = (owner_flat[:, None] == jnp.arange(devices, dtype=jnp.int32)[None, :]).astype(
        jnp.int32
    )
    earlier = jnp.cumsum(one_hot, axis=0) - one_hot
    within = jnp.sum(earlier * one_hot, axis=1)
    return owner_flat * capacity + within


def shards(images, projections, noise_weight, owners, counts):
    devices = lax.axis_size("img")
    local_images, width = images.shape
    candidates = owners.shape[1]
    capacity = 2 * local_images * candidates // devices
    block_dirs = projections.shape[0]
    target = slot_layout(owners, devices, capacity)
    source_rows = jnp.repeat(jnp.arange(local_images, dtype=jnp.int32), candidates)
    outgoing = (
        jnp.zeros((devices * capacity, width), jnp.bfloat16).at[target].set(images[source_rows])
    )
    arrived = lax.all_to_all(
        outgoing.reshape(devices, capacity, width), "img", split_axis=0, concat_axis=0, tiled=True
    ).reshape(devices * capacity, width)
    proj_wide = projections.astype(jnp.float32)
    weighted = (proj_wide * noise_weight[None, :]).astype(jnp.bfloat16)
    power = jnp.sum(proj_wide * proj_wide * noise_weight[None, :], axis=1)
    scores = (
        lax.dot_general(
            arrived, weighted, (((1,), (1,)), ((), ())), preferred_element_type=jnp.float32
        )
        - 0.5 * power[None, :]
    )
    live_slot = jnp.arange(candidates, dtype=jnp.int32)[None, :] < counts[:, None]
    returned = lax.all_to_all(
        scores.reshape(devices, capacity, block_dirs),
        "img",
        split_axis=0,
        concat_axis=0,
        tiled=True,
    ).reshape(devices * capacity, block_dirs)
    mine = returned[target].reshape(local_images, candidates, block_dirs)
    peak_score = jnp.max(jnp.where(live_slot[:, :, None], mine, -jnp.inf), axis=(1, 2))
    shifted = jnp.where(live_slot[:, :, None], jnp.exp(mine - peak_score[:, None, None]), 0.0)
    sum_total = jnp.sum(shifted, axis=(1, 2))
    loglik = peak_score + jnp.log(sum_total)
    posterior = (shifted * (1.0 / sum_total)[:, None, None]).astype(jnp.bfloat16)
    outgoing_post = (
        jnp.zeros((devices * capacity, block_dirs), jnp.bfloat16)
        .at[target]
        .set(posterior.reshape(-1, block_dirs))
    )
    weights_here = lax.all_to_all(
        outgoing_post.reshape(devices, capacity, block_dirs),
        "img",
        split_axis=0,
        concat_axis=0,
        tiled=True,
    ).reshape(devices * capacity, block_dirs)
    backproj = lax.dot_general(
        weights_here, arrived, (((0,), (0,)), ((), ())), preferred_element_type=jnp.float32
    ).astype(jnp.bfloat16)
    weight_sum = jnp.sum(weights_here.astype(jnp.float32), axis=0)
    return (backproj, weight_sum, loglik)


def solution(mesh):
    in_specs = (
        P(("grp", "img"), None),
        P(("grp", "img"), None),
        P("grp"),
        P(("grp", "img"), None),
        P(("grp", "img")),
    )
    out_specs = (P(("grp", "img"), None), P(("grp", "img")), P(("grp", "img")))
    body = line_shards if mesh.shape["img"] == NZ * NY * NC else shards
    return jax.shard_map(body, mesh=mesh, in_specs=in_specs, out_specs=out_specs, check_vma=False)
```

```python
import jax
import jax.numpy as jnp
from jax import lax
from jax.experimental import pallas as pl
from jax.experimental.pallas import tpu as pltpu
from jax.sharding import PartitionSpec as P

NZ, NY, NC = 4, 2, 2
PIECES = 2
LOW = -1e30
TILE_ROWS = 1024


def gather_and_score(
    images, projections, noise, owners, counts,
    gathered_out, post_out, loglik_out,
    held, weighted, power, scores, post, local, stats, mask_out, mask_in, masks, lse,
    load_sem, own_sem, send_sem, recv_sem, store_sem, post_sem,
    mask_send, mask_recv, stat_send, stat_recv,
):
    n = NZ * NY * NC
    me = lax.axis_index("img")
    z, y, c = me // (NY * NC), (me // NC) % NY, me % NC
    rows = images.shape[0]
    piece = rows // PIECES
    block_dirs = projections.shape[0]
    tiles = projections.shape[0] // 128
    pair = NC * rows
    chips = NZ * NY

    def place(zs, ys, cs, h):
        start = ((zs * NY + ys) * NC + cs) * rows + h * piece
        return pl.ds(pl.multiple_of(start, piece), piece)

    loads = [
        pltpu.make_async_copy(
            projections.at[pl.ds(t * 128, 128)], weighted.at[pl.ds(t * 128, 128)], load_sem.at[t]
        )
        for t in range(tiles)
    ]
    for load in loads:
        load.start()
    own_rows = pl.ds(pl.multiple_of(me * rows, rows), rows)
    own_load = pltpu.make_async_copy(images, held.at[own_rows], own_sem)
    own_load.start()

    barrier = pltpu.get_barrier_semaphore()
    peers = [lax.rem(me + k, n) for k in range(1, n)]
    for peer in peers:
        pl.semaphore_signal(barrier, inc=1, device_id={"img": peer})
    pl.semaphore_wait(barrier, n - 1)

    def copies(zs, same_line, h, own, toward):
        ys = y if same_line else 1 - y
        at = place(zs, ys, c, h)
        src = images.at[pl.ds(h * piece, piece)] if own else held.at[at]
        chip = zs * NY + ys
        early = jnp.logical_or(zs == 0, zs == NZ - 1) if h == 1 else None

        def copy(way, peer):
            return pltpu.make_async_remote_copy(
                src_ref=src, dst_ref=held.at[at], send_sem=send_sem.at[chip, h, way],
                recv_sem=recv_sem.at[chip * NC + c, h], device_id={"img": peer},
            )

        out = []
        line_ok = None if same_line else early
        if same_line or early is not None:
            for way, step in ((0, 1), (1, -1)):
                if step in toward:
                    ok = z < NZ - 1 if step == 1 else z > 0
                    if line_ok is not None:
                        ok = jnp.logical_and(ok, line_ok)
                    out.append((ok, copy(way, me + step * NY * NC)))
        if same_line:
            if own or early is None:
                ok = None
            else:
                ok = jnp.logical_not(early)
            out.append((ok, copy(2, me + (1 - 2 * y) * NC)))
        out.append((None, copy(3, me + 1 - 2 * c)))
        return out

    def act(items, do):
        for ok, copy in items:
            if ok is None:
                do(copy)
            else:
                @pl.when(ok)
                def _():
                    do(copy)

    def wait_arrival(zs, ys, cs, h):
        at = place(zs, ys, cs, h)
        pltpu.make_async_remote_copy(
            src_ref=held.at[at], dst_ref=held.at[at], send_sem=send_sem.at[0, 0, 0],
            recv_sem=recv_sem.at[(zs * NY + ys) * NC + cs, h], device_id={"img": me},
        ).wait_recv()

    def source(kind):
        side, same_line, d = kind
        zs = z + side * d
        if d == 0:
            return zs, None
        return zs, (zs >= 0) if side < 0 else (zs <= NZ - 1)

    def toward(kind):
        side, same_line, d = kind
        return (1, -1) if d == 0 else (-side,)

    def guarded(ok, body):
        if ok is None:
            body()
        else:
            pl.when(ok)(body)

    def relay(kind, h):
        zs, ok = source(kind)

        def body():
            wait_arrival(zs, y if kind[1] else 1 - y, c, h)
            act(copies(zs, kind[1], h, False, toward(kind)), lambda copy: copy.start())

        guarded(ok, body)

    def settle(kind, h, own):
        zs, ok = source(kind)

        def body():
            act(copies(zs, kind[1], h, own, toward(kind)), lambda copy: copy.wait_send())

        guarded(ok, body)

    local[...] = jnp.zeros_like(local)
    OWN = (0, True, 0)
    for h in (1, 0):
        act(copies(z, True, h, True, (1, -1)), lambda copy: copy.start())

    owner = lax.broadcasted_iota(jnp.int32, (n, rows), 0)
    count = counts[...].reshape(1, rows)
    live = jnp.zeros((n, rows), jnp.float32)
    for k in range(owners.shape[0]):
        live = live + jnp.where((owners[k:k + 1, :] == owner) & (count > k), 1.0, 0.0)
    none = jnp.zeros_like(live)
    by_owner = jnp.concatenate(
        [jnp.where(c == 0, live, none), jnp.where(c == 0, none, live)], axis=1
    )
    for o in range(n):
        mask_out[o] = jnp.broadcast_to(by_owner[o:o + 1, :], (8, 128))
    mask_in[me] = mask_out[me]

    def mask_copy(peer, k):
        return pltpu.make_async_remote_copy(
            src_ref=mask_out.at[peer], dst_ref=mask_in.at[me], send_sem=mask_send.at[k],
            recv_sem=mask_recv.at[me], device_id={"img": peer},
        )

    for k, peer in enumerate(peers):
        mask_copy(peer, k).start()

    width = projections.shape[1]
    for load in loads:
        load.wait()

    def weigh(t, carry):
        r = pl.ds(pl.multiple_of(t * 32, 32), 32)
        total = jnp.zeros((32, 128), jnp.float32)
        for b in range(width // 128):
            cols = pl.ds(b * 128, 128)
            wide = weighted[r, cols].astype(jnp.float32)
            noise_row = noise[cols].reshape(1, 128)
            total = total + wide * wide * noise_row
            weighted[r, cols] = (wide * noise_row).astype(jnp.bfloat16)
        power[r, :] = jnp.broadcast_to(
            0.5 * jnp.sum(total, axis=1, keepdims=True), (32, 128)
        )
        return carry

    lax.fori_loop(0, block_dirs // 32, weigh, 0)
    own_load.wait()

    def chunk_rows(ch):
        return pl.ds(pl.multiple_of(ch * pair, pair), pair)

    def store(ch):
        at = chunk_rows(ch)
        return pltpu.make_async_copy(held.at[at], gathered_out.at[at], store_sem.at[ch])

    def score(kind):
        zs, ok = source(kind)
        ys = y if kind[1] else 1 - y

        def body():
            for h in range(PIECES):
                wait_arrival(zs, ys, 1 - c, h)
            ch = zs * NY + ys
            store(ch).start()
            at = chunk_rows(ch)

            def first(t, top):
                r = pl.ds(pl.multiple_of(t * TILE_ROWS, TILE_ROWS), TILE_ROWS)
                s = lax.dot_general(
                    weighted[r, :], held[at, :], (((1,), (1,)), ((), ())),
                    preferred_element_type=jnp.float32,
                ) - power[r, :]
                scores[ch, r, :] = s
                return jnp.maximum(top, jnp.max(s, axis=0, keepdims=True))

            top = lax.fori_loop(
                0, block_dirs // TILE_ROWS, first, jnp.full((1, pair), LOW, jnp.float32)
            )

            def second(t, total):
                r = pl.ds(pl.multiple_of(t * 256, 256), 256)
                e = jnp.exp(scores[ch, r, :] - top)
                scores[ch, r, :] = e
                return total + jnp.sum(e, axis=0, keepdims=True)

            total = lax.fori_loop(
                0, block_dirs // 256, second, jnp.zeros((1, pair), jnp.float32)
            )
            local[0, pl.ds(ch, 1), :] = top
            local[1, pl.ds(ch, 1), :] = total

        guarded(ok, body)

    def offer():
        for k, peer in enumerate(peers):
            pltpu.make_async_remote_copy(
                src_ref=mask_in.at[peer], dst_ref=mask_in.at[peer],
                send_sem=mask_send.at[k], recv_sem=mask_recv.at[peer],
                device_id={"img": me},
            ).wait_recv()
        for ch in range(chips):
            masks[ch:ch + 1, :] = mask_in[ch * NC][0:1, :] + mask_in[ch * NC + 1][0:1, :]
        is_live = masks[...] > 0.5
        stats[me, 0] = jnp.where(is_live, local[0], LOW)
        stats[me, 1] = jnp.where(is_live, local[1], 0.0)
        for k, peer in enumerate(peers):
            stat_copy(peer, k).start()

    def stat_copy(peer, k):
        return pltpu.make_async_remote_copy(
            src_ref=stats.at[me], dst_ref=stats.at[me],
            send_sem=stat_send.at[k], recv_sem=stat_recv.at[me],
            device_id={"img": peer},
        )

    def post_copy(ch):
        return pltpu.make_async_copy(
            post.at[ch], post_out.at[:, pl.ds(ch * pair, pair)], post_sem.at[ch]
        )

    def conclude(chunks):
        for k, peer in enumerate(peers):
            pltpu.make_async_remote_copy(
                src_ref=stats.at[peer], dst_ref=stats.at[peer],
                send_sem=stat_send.at[k], recv_sem=stat_recv.at[peer],
                device_id={"img": me},
            ).wait_recv()
        peak = stats[0, 0]
        for o in range(1, n):
            peak = jnp.maximum(peak, stats[o, 0])
        total = jnp.zeros_like(peak)
        for o in range(n):
            total = total + stats[o, 1] * jnp.exp(stats[o, 0] - peak)
        inverse = 1.0 / total
        scale = jnp.where(masks[...] > 0.5, jnp.exp(stats[me, 0] - peak) * inverse, 0.0)
        logs = peak + jnp.log(total)
        for ch in chunks:
            lse[ch:ch + 1, :] = logs[ch:ch + 1, :]
        for ch in chunks:
            row = scale[ch:ch + 1, :]

            def weights(t, carry):
                r = pl.ds(pl.multiple_of(t * 256, 256), 256)
                post[ch, r, :] = (scores[ch, r, :] * row).astype(jnp.bfloat16)
                return carry

            lax.fori_loop(0, block_dirs // 256, weights, 0)
            post_copy(ch).start()

    L, R = -1, 1
    ACROSS = (0, False, 0)
    relay(ACROSS, 1)
    relay((L, True, 1), 1)
    relay((R, True, 1), 1)
    score(OWN)
    relay(ACROSS, 0)
    relay((L, True, 1), 0)
    relay((R, True, 1), 0)
    score(ACROSS)
    relay((L, True, 2), 1)
    relay((R, True, 2), 1)
    score((L, True, 1))
    relay((L, True, 2), 0)
    relay((R, True, 2), 0)
    score((R, True, 1))
    for h in (1, 0):
        for side in (L, R):
            relay((side, False, 1), h)
    score((L, True, 2))
    score((R, True, 2))
    score((L, False, 1))
    score((R, False, 1))
    for h in (1, 0):
        for side in (L, R):
            relay((side, True, 3), h)
    for h in (1, 0):
        for side in (L, R):
            relay((side, False, 2), h)
    score((L, False, 2))
    score((R, False, 2))
    score((L, True, 3))
    score((R, True, 3))
    for h in range(PIECES):
        settle(OWN, h, True)
        settle(ACROSS, h, False)
        for d in (1, 2):
            for side in (L, R):
                for line in (True, False):
                    settle((side, line, d), h, False)
    for h in (1, 0):
        for side in (L, R):
            relay((side, False, 3), h)
    score((L, False, 3))
    score((R, False, 3))
    offer()
    for h in range(PIECES):
        for side in (L, R):
            settle((side, True, 3), h, False)
            settle((side, False, 3), h, False)
    for k, peer in enumerate(peers):
        mask_copy(peer, k).wait_send()
    for ch in range(chips):
        store(ch).wait()
    conclude(range(chips))
    mine = lse[pl.ds(z * NY + y, 1), :]
    loglik_out[...] = jnp.where(c == 0, mine[:, :rows], mine[:, rows:]).reshape(rows)
    for k, peer in enumerate(peers):
        stat_copy(peer, k).wait_send()
    for ch in range(chips):
        post_copy(ch).wait()


BACK_ROWS, BACK_COLS = 512, 512


def back(post, gathered, loglik, out, wsum_out, loglik_out, weights, held, total, sems, out_sems):
    dirs, depth = weights.shape
    width = held.shape[1]
    spans = [(b, min(BACK_COLS, width - b)) for b in range(0, width, BACK_COLS)]
    first = pltpu.make_async_copy(post, weights, sems.at[len(spans)])
    first.start()
    loads, saves = [], []
    for j, (b, size) in enumerate(spans):
        cols = pl.ds(b, size)
        loads.append(pltpu.make_async_copy(gathered.at[:, cols], held.at[:, cols], sems.at[j]))
        saves.append(pltpu.make_async_copy(total.at[:, cols], out.at[:, cols], out_sems.at[j]))
    for load in loads:
        load.start()
    loglik_out[...] = loglik[...]
    first.wait()
    for j, (b, size) in enumerate(spans):
        loads[j].wait()

        for t in range(0, dirs, BACK_ROWS):
            total[t:t + BACK_ROWS, b:b + size] = jnp.dot(
                weights[t:t + BACK_ROWS, :], held[:, b:b + size],
                preferred_element_type=jnp.float32,
            ).astype(jnp.bfloat16)
        saves[j].start()
    for t in range(dirs // 128):
        part = jnp.zeros((128, 128), jnp.float32)
        for k in range(depth // 128):
            part = part + weights[t * 128:(t + 1) * 128, k * 128:(k + 1) * 128].astype(jnp.float32)
        wsum_out[t * 128:(t + 1) * 128] = jnp.sum(jnp.transpose(part), axis=0)
    for save in saves:
        save.wait()


def line_shards(images, projections, noise_weight, owners, counts):
    rows, width = images.shape
    dirs = projections.shape[0]
    n = NZ * NY * NC
    chips = NZ * NY
    pair = NC * rows
    hbm = pl.BlockSpec(memory_space=pl.ANY)
    vmem = pl.BlockSpec(memory_space=pltpu.VMEM)
    dma = pltpu.SemaphoreType.DMA
    gathered, post, loglik = pl.pallas_call(
        gather_and_score,
        out_shape=(
            jax.ShapeDtypeStruct((n * rows, width), jnp.bfloat16),
            jax.ShapeDtypeStruct((dirs, n * rows), jnp.bfloat16),
            jax.ShapeDtypeStruct((rows,), jnp.float32),
        ),
        in_specs=[hbm, hbm, vmem, vmem, vmem],
        out_specs=(hbm, hbm, vmem),
        scratch_shapes=[
            pltpu.VMEM((n * rows, width), jnp.bfloat16),
            pltpu.VMEM((dirs, width), jnp.bfloat16),
            pltpu.VMEM((dirs, 128), jnp.float32),
            pltpu.VMEM((chips, dirs, pair), jnp.float32),
            pltpu.VMEM((chips, dirs, pair), jnp.bfloat16),
            pltpu.VMEM((2, chips, pair), jnp.float32),
            pltpu.VMEM((n, 2, chips, pair), jnp.float32),
            pltpu.VMEM((n, 8, 128), jnp.float32),
            pltpu.VMEM((n, 8, 128), jnp.float32),
            pltpu.VMEM((chips, pair), jnp.float32),
            pltpu.VMEM((chips, pair), jnp.float32),
            dma((dirs // 128,)),
            dma(()),
            dma((chips, PIECES, 4)),
            dma((n, PIECES)),
            dma((chips,)),
            dma((chips,)),
            dma((n - 1,)),
            dma((n,)),
            dma((n - 1,)),
            dma((n,)),
        ],
        compiler_params=pltpu.CompilerParams(
            collective_id=0, has_side_effects=True, vmem_limit_bytes=56 * 1024 * 1024
        ),
        cost_estimate=pl.CostEstimate(
            flops=2 * dirs * n * rows * width, bytes_accessed=20_000_000,
            transcendentals=dirs * n * rows,
        ),
        name="gather_and_score",
    )(images, projections, noise_weight, owners.T, counts)
    spans = -(-width // BACK_COLS)
    return pl.pallas_call(
        back,
        out_shape=(
            jax.ShapeDtypeStruct((dirs, width), jnp.bfloat16),
            jax.ShapeDtypeStruct((dirs,), jnp.float32),
            jax.ShapeDtypeStruct((rows,), jnp.float32),
        ),
        in_specs=[hbm, hbm, vmem],
        out_specs=(hbm, vmem, vmem),
        scratch_shapes=[
            pltpu.VMEM((dirs, n * rows), jnp.bfloat16),
            pltpu.VMEM((n * rows, width), jnp.bfloat16),
            pltpu.VMEM((dirs, width), jnp.bfloat16),
            dma((spans + 1,)),
            dma((spans,)),
        ],
        compiler_params=pltpu.CompilerParams(vmem_limit_bytes=56 * 1024 * 1024),
        cost_estimate=pl.CostEstimate(
            flops=2 * dirs * n * rows * width, bytes_accessed=16_000_000, transcendentals=0
        ),
        name="back",
    )(post, gathered, loglik)


def slot_layout(owners, devices, capacity):
    owner_flat = owners.reshape(-1)
    one_hot = (owner_flat[:, None] == jnp.arange(devices, dtype=jnp.int32)[None, :]).astype(
        jnp.int32
    )
    earlier = jnp.cumsum(one_hot, axis=0) - one_hot
    within = jnp.sum(earlier * one_hot, axis=1)
    return owner_flat * capacity + within


def shards(images, projections, noise_weight, owners, counts):
    devices = lax.axis_size("img")
    local_images, width = images.shape
    candidates = owners.shape[1]
    capacity = 2 * local_images * candidates // devices
    block_dirs = projections.shape[0]
    target = slot_layout(owners, devices, capacity)
    source_rows = jnp.repeat(jnp.arange(local_images, dtype=jnp.int32), candidates)
    outgoing = (
        jnp.zeros((devices * capacity, width), jnp.bfloat16).at[target].set(images[source_rows])
    )
    arrived = lax.all_to_all(
        outgoing.reshape(devices, capacity, width), "img", split_axis=0, concat_axis=0, tiled=True
    ).reshape(devices * capacity, width)
    proj_wide = projections.astype(jnp.float32)
    weighted = (proj_wide * noise_weight[None, :]).astype(jnp.bfloat16)
    power = jnp.sum(proj_wide * proj_wide * noise_weight[None, :], axis=1)
    scores = (
        lax.dot_general(
            arrived, weighted, (((1,), (1,)), ((), ())), preferred_element_type=jnp.float32
        )
        - 0.5 * power[None, :]
    )
    live_slot = jnp.arange(candidates, dtype=jnp.int32)[None, :] < counts[:, None]
    returned = lax.all_to_all(
        scores.reshape(devices, capacity, block_dirs),
        "img",
        split_axis=0,
        concat_axis=0,
        tiled=True,
    ).reshape(devices * capacity, block_dirs)
    mine = returned[target].reshape(local_images, candidates, block_dirs)
    peak_score = jnp.max(jnp.where(live_slot[:, :, None], mine, -jnp.inf), axis=(1, 2))
    shifted = jnp.where(live_slot[:, :, None], jnp.exp(mine - peak_score[:, None, None]), 0.0)
    sum_total = jnp.sum(shifted, axis=(1, 2))
    loglik = peak_score + jnp.log(sum_total)
    posterior = (shifted * (1.0 / sum_total)[:, None, None]).astype(jnp.bfloat16)
    outgoing_post = (
        jnp.zeros((devices * capacity, block_dirs), jnp.bfloat16)
        .at[target]
        .set(posterior.reshape(-1, block_dirs))
    )
    weights_here = lax.all_to_all(
        outgoing_post.reshape(devices, capacity, block_dirs),
        "img",
        split_axis=0,
        concat_axis=0,
        tiled=True,
    ).reshape(devices * capacity, block_dirs)
    backproj = lax.dot_general(
        weights_here, arrived, (((0,), (0,)), ((), ())), preferred_element_type=jnp.float32
    ).astype(jnp.bfloat16)
    weight_sum = jnp.sum(weights_here.astype(jnp.float32), axis=0)
    return (backproj, weight_sum, loglik)


def solution(mesh):
    in_specs = (
        P(("grp", "img"), None),
        P(("grp", "img"), None),
        P("grp"),
        P(("grp", "img"), None),
        P(("grp", "img")),
    )
    out_specs = (P(("grp", "img"), None), P(("grp", "img")), P(("grp", "img")))
    body = line_shards if mesh.shape["img"] == NZ * NY * NC else shards
    return jax.shard_map(body, mesh=mesh, in_specs=in_specs, out_specs=out_specs, check_vma=False)
```
